256 devices in a mesh: rep: 32 (over z, x), sub: 8 (over y, core).
Axes of the slice: x: 4, y: 4, z: 8, core: 2. Of those that a mesh axis runs over, the one named last changes fastest.
Arguments:
- pre_act: bfloat16 [150528, 4096], P(('rep', 'sub')), may hold values from -6 to 6
- upstream: bfloat16 [150528, 1024], P(('rep', 'sub')), may hold values from -0.24707031 to 0.24707031
- layer_scale: float32 [1024], replicated, may hold values from 0.25 to 4
- initial_q: float32 [8, 1024], replicated, may hold values from -6 to 6
Outputs:
- basis_out: float32 [8, 4096], replicated
- q_out: float32 [8, 1024], replicated
- residual: bfloat16 [1048576, 1024], P(('rep', 'sub'))
The draws below stay inside these ranges and needn't reach their ends.
All inputs are finite; a program needn't handle non-finite values.
Results may differ from the reference program's by a relative error of at most 0.0061.
Values sent between devices are 32-bit elements; how exact they have to be, the bound alone decides.
No kernel may reach another device: no remote copies, remote signals or barrier semaphores. Data moves between devices by JAX's collectives and lax.ppermute only.
A program may use at most 128 MiB of HBM per device.

```python
import math
import jax
import jax.numpy as jnp
from jax import lax

WIDTH = 1024
HIDDEN_SIZE = 4096
RANK = 8
PIX = 49
IMG_DEV = 12
ROWS_DEV = 588
ROWS = 150528
N_REP = 32
N_SUB = 8


def block_scale(rng, dims, cuts, smallest, largest):
    level, own = 1.0, jax.random.fold_in(rng, 6)
    for dim, parts in cuts:
        steps = jnp.exp(jax.random.uniform(jax.random.fold_in(own, dim), (parts,), jnp.float32, smallest / len(cuts), largest / len(cuts)))
        level = level * jnp.repeat(steps, dims[dim] // parts).reshape([-1 if axis == dim else 1 for axis in range(len(dims))])
    return level


def centred(stream_key, dims, width, reach, cuts=(), dtype=jnp.bfloat16):
    values = width * jax.random.normal(stream_key, dims, jnp.float32)
    if cuts:
        values = values * block_scale(stream_key, dims, cuts, -0.22, 0.18)
    return jnp.clip(values, -reach, reach).astype(dtype)


def setup_inputs(seed: int = 0) -> dict:
    arg_keys = jax.random.split(jax.random.key(seed), 5)
    return {
        "pre_act": centred(arg_keys[0], (ROWS, HIDDEN_SIZE), 1.0, 6.0, ((0, 256),)),
        "upstream": centred(arg_keys[1], (ROWS, WIDTH), (1.0 / (IMG_DEV * PIX) ** 0.5), 0.24707031, ((0, 256),)),
        "layer_scale": jnp.clip(jnp.exp(jax.random.uniform(arg_keys[2], (WIDTH,), jnp.float32, math.log(0.25), math.log(4.0))), 0.25, 4.0),
        "initial_q": centred(arg_keys[3], (RANK, WIDTH), 1.0, 6.0, (), jnp.float32),
    }


def reference(pre_act, upstream, layer_scale, initial_q):
    highest = lax.Precision.HIGHEST
    devices = N_REP * N_SUB
    activated = jax.nn.gelu(pre_act.astype(jnp.float32), approximate=False).astype(jnp.bfloat16)
    scaled = (upstream.astype(jnp.float32) * layer_scale[None, :]).astype(jnp.bfloat16)
    reduced = jnp.dot(initial_q, scaled.astype(jnp.float32).T, precision=highest)
    p_total = jnp.dot(reduced, activated.astype(jnp.float32), precision=highest)
    gram_matrix = jnp.dot(p_total, p_total.T, precision=highest)
    chol_lower = jnp.linalg.cholesky(gram_matrix)
    ortho_basis = jax.scipy.linalg.solve_triangular(chol_lower, p_total, lower=True)
    act_blocks = activated.reshape(devices, ROWS_DEV, HIDDEN_SIZE)
    scl_blocks = scaled.reshape(devices, ROWS_DEV, WIDTH)

    def per_device(pair):
        act_rows, scl_rows = pair
        gradient = jnp.dot(act_rows.astype(jnp.float32).T, scl_rows.astype(jnp.float32), precision=highest)
        q_local = jnp.dot(ortho_basis, gradient, precision=highest)
        approx = jnp.dot(ortho_basis.T, q_local, precision=highest)
        return (q_local, (gradient - approx).astype(jnp.bfloat16))
    q_parts, resid_blocks = lax.map(per_device, (act_blocks, scl_blocks))
    q_total = jnp.sum(q_parts, axis=0)
    basis_out = ortho_basis * jnp.float32(HIDDEN_SIZE ** 0.5)
    q_out = q_total / jnp.float32(devices ** 0.5)
    return (basis_out, q_out, resid_blocks.reshape(devices * HIDDEN_SIZE, WIDTH))
```

```python
import functools
import math

import jax
import jax.numpy as jnp
from jax import lax
from jax.experimental import pallas as pl
from jax.experimental.pallas import tpu as pltpu
from jax.sharding import Mesh
from jax.sharding import PartitionSpec as P

f32, bf16 = jnp.float32, jnp.bfloat16
ROWS, HID, WID, RANK, LANES = 588, 4096, 1024, 8, 128
PLANE = ("x", "y", "c")


def split3(v):
    a = v.astype(bf16)
    r = v - a.astype(f32)
    b = r.astype(bf16)
    c = (r - b.astype(f32)).astype(bf16)
    return jnp.concatenate([a, b, c], axis=0)


def fold3(v):
    return v[0:RANK] + v[RANK : 2 * RANK] + v[2 * RANK : 3 * RANK]


def gelu(v):
    return 0.5 * v * (1.0 + lax.erf(v * math.sqrt(0.5)))


def front_kernel(cols, slab, pre, up, scale, q, act, scaled, p_out, reduced):
    @pl.when(pl.program_id(0) == 0)
    def _():
        scaled[...] = (up[...].astype(f32) * scale[...]).astype(bf16)
        r = lax.dot_general(
            split3(q[...]), scaled[...], (((1,), (1,)), ((), ())), preferred_element_type=f32
        )
        reduced[...] = split3(fold3(r))

    full = ROWS // slab

    def step(i, carry):
        rows = pl.ds(pl.multiple_of(i * slab, slab), slab)
        act[rows, :] = gelu(pre[rows, :].astype(f32)).astype(bf16)
        return carry

    lax.fori_loop(0, full, step, 0)
    act[full * slab : ROWS, :] = gelu(pre[full * slab : ROWS, :].astype(f32)).astype(bf16)
    part = fold3(jnp.dot(reduced[...], act[...], preferred_element_type=f32))
    for j in range(cols // LANES):
        p_out[j] = part[:, j * LANES : (j + 1) * LANES]


def front(pre, up, scale, q, cols=1024, slab=16):
    return pl.pallas_call(
        functools.partial(front_kernel, cols, slab),
        grid=(HID // cols,),
        in_specs=[
            pl.BlockSpec((ROWS, cols), lambda i: (0, i)),
            pl.BlockSpec((ROWS, WID), lambda i: (0, 0)),
            pl.BlockSpec((1, WID), lambda i: (0, 0)),
            pl.BlockSpec((RANK, WID), lambda i: (0, 0)),
        ],
        out_specs=[
            pl.BlockSpec((ROWS, cols), lambda i: (0, i)),
            pl.BlockSpec((ROWS, WID), lambda i: (0, 0)),
            pl.BlockSpec((cols // LANES, RANK, LANES), lambda i: (i, 0, 0)),
        ],
        out_shape=[
            jax.ShapeDtypeStruct((ROWS, HID), bf16),
            jax.ShapeDtypeStruct((ROWS, WID), bf16),
            jax.ShapeDtypeStruct((HID // LANES, RANK, LANES), f32),
        ],
        scratch_shapes=[pltpu.VMEM((3 * RANK, ROWS), bf16)],
        compiler_params=pltpu.CompilerParams(vmem_limit_bytes=24 << 20),
        cost_estimate=pl.CostEstimate(flops=60 * ROWS * HID, bytes_accessed=10 << 20, transcendentals=ROWS * HID),
        name="front",
    )(pre, up, scale, q)


def project_kernel(act, scaled, p, u_out):
    flat = jnp.concatenate([p[j] for j in range(HID // LANES)], axis=1)
    c = lax.dot_general(
        split3(flat), act[...], (((1,), (1,)), ((), ())), preferred_element_type=f32
    )
    u = fold3(jnp.dot(split3(fold3(c)), scaled[...], preferred_element_type=f32))
    for j in range(WID // LANES):
        u_out[j] = u[:, j * LANES : (j + 1) * LANES]


def project(act, scaled, p):
    return pl.pallas_call(
        project_kernel,
        out_shape=jax.ShapeDtypeStruct((WID // LANES, RANK, LANES), f32),
        compiler_params=pltpu.CompilerParams(vmem_limit_bytes=24 << 20),
        cost_estimate=pl.CostEstimate(flops=48 * ROWS * HID, bytes_accessed=6 << 20, transcendentals=0),
        name="project",
    )(act, scaled, p)


def ortho_kernel(p, u, basis, inverse, lhs, rhs):
    flat = jnp.concatenate([p[j] for j in range(HID // LANES)], axis=1)
    parts = split3(flat)
    g = lax.dot_general(parts, parts, (((1,), (1,)), ((), ())), preferred_element_type=f32)
    g = fold3(g)
    gram = g[:, 0:RANK] + g[:, RANK : 2 * RANK] + g[:, 2 * RANK : 3 * RANK]
    row = lax.broadcasted_iota(jnp.int32, (RANK, RANK), 0)
    col = lax.broadcasted_iota(jnp.int32, (RANK, RANK), 1)
    inv = jnp.where(row == col, 1.0, 0.0).astype(f32)
    for j in range(RANK):
        root = lax.rsqrt(gram[j : j + 1, j : j + 1])
        gram_row, inv_row = gram[j : j + 1, :] * root, inv[j : j + 1, :] * root
        factor = jnp.where(row[:, 0:1] > j, gram[:, j : j + 1] * root, 0.0)
        gram = jnp.where(row == j, gram_row, gram - factor * gram_row)
        inv = jnp.where(row == j, inv_row, inv - factor * inv_row)
    o = jnp.dot(inv, flat, precision=lax.Precision.HIGHEST, preferred_element_type=f32)
    u_flat = jnp.concatenate([u[j] for j in range(WID // LANES)], axis=1)
    q = jnp.dot(inv, u_flat, precision=lax.Precision.HIGHEST, preferred_element_type=f32)
    basis[...] = o * math.sqrt(HID)
    inverse[...] = inv
    o_hi = o.astype(bf16)
    o_lo = (o - o_hi.astype(f32)).astype(bf16)
    q_hi = q.astype(bf16)
    q_lo = (q - q_hi.astype(f32)).astype(bf16)
    lhs[...] = jnp.concatenate([o_hi, o_hi, o_lo], axis=0)
    rhs[...] = jnp.concatenate([q_hi, q_lo, q_hi], axis=0)


def ortho(p, u):
    return pl.pallas_call(
        ortho_kernel,
        out_shape=[
            jax.ShapeDtypeStruct((RANK, HID), f32),
            jax.ShapeDtypeStruct((RANK, RANK), f32),
            jax.ShapeDtypeStruct((3 * RANK, HID), bf16),
            jax.ShapeDtypeStruct((3 * RANK, WID), bf16),
        ],
        compiler_params=pltpu.CompilerParams(vmem_limit_bytes=8 << 20),
        cost_estimate=pl.CostEstimate(flops=1 << 24, bytes_accessed=1 << 20, transcendentals=0),
        name="ortho",
    )(p, u)


def residual_kernel(act, scaled, lhs, rhs, out):
    contract = (((0,), (0,)), ((), ()))
    acc = lax.dot_general(act[...], scaled[...], contract, preferred_element_type=f32)
    low = lax.dot_general(lhs[...], rhs[...], contract, preferred_element_type=f32)
    out[...] = (acc - low).astype(bf16)


def residual_of(act, scaled, lhs, rhs, rows=512):
    return pl.pallas_call(
        residual_kernel,
        grid=(HID // rows,),
        in_specs=[
            pl.BlockSpec((ROWS, rows), lambda i: (0, i)),
            pl.BlockSpec((ROWS, WID), lambda i: (0, 0)),
            pl.BlockSpec((3 * RANK, rows), lambda i: (0, i)),
            pl.BlockSpec((3 * RANK, WID), lambda i: (0, 0)),
        ],
        out_specs=pl.BlockSpec((rows, WID), lambda i: (i, 0)),
        out_shape=jax.ShapeDtypeStruct((HID, WID), bf16),
        compiler_params=pltpu.CompilerParams(vmem_limit_bytes=24 << 20),
        cost_estimate=pl.CostEstimate(flops=2 * ROWS * HID * WID, bytes_accessed=14 << 20, transcendentals=0),
        name="residual",
    )(act, scaled, lhs, rhs)


def finish_kernel(inverse, u, q_out, *, devices):
    flat = jnp.concatenate([u[j] for j in range(WID // LANES)], axis=1)
    q = jnp.dot(inverse[...], flat, precision=lax.Precision.HIGHEST, preferred_element_type=f32)
    q_out[...] = q * (1.0 / math.sqrt(devices))


def finish(inverse, u, devices):
    return pl.pallas_call(
        functools.partial(finish_kernel, devices=devices),
        out_shape=jax.ShapeDtypeStruct((RANK, WID), f32),
        compiler_params=pltpu.CompilerParams(vmem_limit_bytes=4 << 20),
        name="finish",
    )(inverse, u)


def exchange(v, axis, partner):
    n = lax.axis_size(axis)
    return v + lax.ppermute(v, axis, [(i, partner(i, n)) for i in range(n)])


def even_pair(i, n):
    return i ^ 1


def odd_pair(i, n):
    return (i + 1) % n if i % 2 else (i - 1) % n


def far_pair(i, n):
    return {1: 6, 6: 1, 2: 5, 5: 2, 3: 0, 0: 3, 4: 7, 7: 4}[i]


def reduce_all_to_all(v, axes, n):
    got = lax.all_to_all(v, axes, 0, 0, tiled=True)
    return jnp.sum(got.reshape((n, v.shape[0] // n) + v.shape[1:]), axis=0)


def gather_all_to_all(v, axes, n):
    copies = jnp.broadcast_to(v[None], (n,) + v.shape).reshape((n * v.shape[0],) + v.shape[1:])
    return lax.all_to_all(copies, axes, 0, 0, tiled=True)


def body(pre_act, upstream, layer_scale, initial_q):
    act, scaled, p_local = front(pre_act, upstream, layer_scale.reshape(1, WID), initial_q)
    with jax.named_scope("sum_p"):
        part = reduce_all_to_all(p_local, PLANE, 32)
        part = jnp.sum(gather_all_to_all(part, "z", 8), axis=0, keepdims=True)
        p_total = gather_all_to_all(part, PLANE, 32)
    u = project(act, scaled, p_total)
    basis_out, inverse, lhs, rhs = ortho(p_total, u)
    residual = residual_of(act, scaled, lhs, rhs)
    with jax.named_scope("sum_u"):
        t = exchange(u, "c", even_pair)
        for axis in ("y", "x", "z"):
            t = exchange(t, axis, even_pair)
            t = exchange(t, axis, odd_pair)
        t = exchange(t, "z", far_pair)
    q_out = finish(inverse, t, 256)
    return (basis_out, q_out, residual)


def solution(mesh):
    fine = Mesh(mesh.devices.reshape(8, 4, 4, 2), ("z", "x", "y", "c"))
    split = P(("z", "x", "y", "c"), None)
    return jax.shard_map(
        body, mesh=fine, in_specs=(split, split, P(), P()), out_specs=(P(), P(), split), check_vma=False
    )
```

```python
import functools
import math

import jax
import jax.numpy as jnp
from jax import lax
from jax.experimental import pallas as pl
from jax.experimental.pallas import tpu as pltpu
from jax.sharding import Mesh
from jax.sharding import PartitionSpec as P

f32, bf16 = jnp.float32, jnp.bfloat16
ROWS, HID, WID, RANK, LANES = 588, 4096, 1024, 8, 128
EVEN, AUG = 592, 624
SPLIT = 3
FRONT_LIMIT = 52 << 20
RES_LIMIT = 50 << 20
PIECE_FLOPS = 2 * ROWS * HID * WID // 8
PLANE = ("x", "y", "c")


def split3(v):
    a = v.astype(bf16)
    r = v - a.astype(f32)
    b = r.astype(bf16)
    c = (r - b.astype(f32)).astype(bf16)
    return jnp.concatenate([a, b, c], axis=0)


def fold3(v):
    return v[0:RANK] + v[RANK : 2 * RANK] + v[2 * RANK : 3 * RANK]


def gelu(v):
    return 0.5 * v * (1.0 + lax.erf(v * math.sqrt(0.5)))


def front_kernel(chunks, cols, slab, pre_h, up_h, scale_h, q_h, act, act_h, scaled, p_out, pre, up, scale, q, reduced, sem, sem_s, sem_o):
    wide = HID // chunks

    def load(c):
        where = (slice(None), slice(c * wide, (c + 1) * wide))
        return pltpu.make_async_copy(pre_h.at[where], pre.at[where], sem.at[c])

    small = [
        pltpu.make_async_copy(q_h, q, sem_s.at[0]),
        pltpu.make_async_copy(scale_h, scale, sem_s.at[1]),
        pltpu.make_async_copy(up_h, up, sem_s.at[2]),
    ]
    load(0).start()
    for copy in small:
        copy.start()
    for c in range(1, chunks):
        load(c).start()
    act[EVEN - 16 : EVEN, :] = jnp.zeros((16, HID), bf16)
    scaled[EVEN - 16 : EVEN, :] = jnp.zeros((16, WID), bf16)

    def store(c):
        where = (slice(None), slice(c * wide, (c + 1) * wide))
        return pltpu.make_async_copy(act.at[where], act_h.at[where], sem_o.at[c])

    def activate(first):
        for r in range(0, ROWS, slab):
            rows, at = slice(r, min(r + slab, ROWS)), slice(first, first + cols)
            act[rows, at] = gelu(pre[rows, at].astype(f32)).astype(bf16)

    def multiply(first):
        part = fold3(jnp.dot(reduced[...], act[:, first : first + cols], preferred_element_type=f32))
        for j in range(cols // LANES):
            p_out[first // LANES + j] = part[:, j * LANES : (j + 1) * LANES]

    for c in range(chunks):
        load(c).wait()
        for first in range(c * wide, (c + 1) * wide, cols):
            activate(first)
            if first == 0:
                for copy in small:
                    copy.wait()
                for r in range(0, ROWS, 64):
                    rows = slice(r, min(r + 64, ROWS))
                    scaled[rows, :] = (up[rows, :].astype(f32) * scale[...]).astype(bf16)
                r = lax.dot_general(
                    split3(q[...]), scaled[...], (((1,), (1,)), ((), ())), preferred_element_type=f32
                )
                reduced[...] = split3(fold3(r))
            else:
                multiply(first - cols)
        store(c).start()
    multiply(HID - cols)
    for c in range(chunks):
        store(c).wait()


def front(pre, up, scale, q, chunks=8, cols=256, slab=16):
    return pl.pallas_call(
        functools.partial(front_kernel, chunks, cols, slab),
        in_specs=[pl.BlockSpec(memory_space=pl.ANY)] * 4,
        out_specs=[pl.BlockSpec(memory_space=pltpu.VMEM if i != 1 else pl.ANY) for i in range(4)],
        out_shape=[
            pltpu.VMEM((EVEN, HID), bf16),
            pltpu.HBM((EVEN, HID), bf16),
            pltpu.VMEM((EVEN, WID), bf16),
            pltpu.VMEM((HID // LANES, RANK, LANES), f32),
        ],
        scratch_shapes=[
            pltpu.VMEM((ROWS, HID), bf16),
            pltpu.VMEM((ROWS, WID), bf16),
            pltpu.VMEM((1, WID), f32),
            pltpu.VMEM((RANK, WID), f32),
            pltpu.VMEM((3 * RANK, EVEN), bf16),
            pltpu.SemaphoreType.DMA((chunks,)),
            pltpu.SemaphoreType.DMA((3,)),
            pltpu.SemaphoreType.DMA((chunks,)),
        ],
        compiler_params=pltpu.CompilerParams(vmem_limit_bytes=FRONT_LIMIT),
        cost_estimate=pl.CostEstimate(flops=60 * ROWS * HID, bytes_accessed=10 << 20, transcendentals=ROWS * HID),
        name="front",
    )(pre, up, scale, q)


def project_kernel(act, scaled, p, u_out, keep, send):
    flat = jnp.concatenate([p[j] for j in range(HID // LANES)], axis=1)
    c = lax.dot_general(
        split3(flat), act[...], (((1,), (1,)), ((), ())), preferred_element_type=f32
    )
    u = fold3(jnp.dot(split3(fold3(c)), scaled[...], preferred_element_type=f32))
    core = lax.axis_index("c")
    half = WID // LANES // 2
    for j in range(half):
        low, high = (u[:, k * LANES : (k + 1) * LANES] for k in (j, half + j))
        u_out[j] = low
        u_out[half + j] = high
        keep[j] = jnp.where(core == 0, low, high)
        send[j] = jnp.where(core == 0, high, low)


def project(act, scaled, p):
    n = WID // LANES
    return pl.pallas_call(
        project_kernel,
        in_specs=[pl.BlockSpec(memory_space=pltpu.VMEM)] * 3,
        out_specs=[pl.BlockSpec(memory_space=pltpu.VMEM)] * 3,
        out_shape=[jax.ShapeDtypeStruct((k, RANK, LANES), f32) for k in (n, n // 2, n // 2)],
        compiler_params=pltpu.CompilerParams(vmem_limit_bytes=16 << 20),
        cost_estimate=pl.CostEstimate(flops=48 * ROWS * HID, bytes_accessed=6 << 20, transcendentals=0),
        name="project",
    )(act, scaled, p)


def ortho_kernel(p, u, scaled, basis, inverse, lhs, rhs):
    flat = jnp.concatenate([p[j] for j in range(HID // LANES)], axis=1)
    parts = split3(flat)
    g = lax.dot_general(parts, parts, (((1,), (1,)), ((), ())), preferred_element_type=f32)
    g = fold3(g)
    gram = g[:, 0:RANK] + g[:, RANK : 2 * RANK] + g[:, 2 * RANK : 3 * RANK]
    row = lax.broadcasted_iota(jnp.int32, (RANK, RANK), 0)
    col = lax.broadcasted_iota(jnp.int32, (RANK, RANK), 1)
    inv = jnp.where(row == col, 1.0, 0.0).astype(f32)
    for j in range(RANK):
        root = lax.rsqrt(gram[j : j + 1, j : j + 1])
        gram_row, inv_row = gram[j : j + 1, :] * root, inv[j : j + 1, :] * root
        factor = jnp.where(row[:, 0:1] > j, gram[:, j : j + 1] * root, 0.0)
        gram = jnp.where(row == j, gram_row, gram - factor * gram_row)
        inv = jnp.where(row == j, inv_row, inv - factor * inv_row)
    o = jnp.dot(inv, flat, precision=lax.Precision.HIGHEST, preferred_element_type=f32)
    u_flat = jnp.concatenate([u[j] for j in range(WID // LANES)], axis=1)
    q = jnp.dot(inv, u_flat, precision=lax.Precision.HIGHEST, preferred_element_type=f32)
    basis[...] = o * math.sqrt(HID)
    inverse[...] = inv
    o_hi = (-o).astype(bf16)
    o_lo = (-o - o_hi.astype(f32)).astype(bf16)
    q_hi = q.astype(bf16)
    q_lo = (q - q_hi.astype(f32)).astype(bf16)
    lhs[...] = jnp.concatenate([o_hi, o_hi, o_lo, o_lo], axis=0)
    rhs[0:EVEN, :] = scaled[...]
    rhs[EVEN:AUG, :] = jnp.concatenate([q_hi, q_lo, q_hi, q_lo], axis=0)


def ortho(p, u, scaled):
    return pl.pallas_call(
        ortho_kernel,
        out_shape=[
            jax.ShapeDtypeStruct((RANK, HID), f32),
            jax.ShapeDtypeStruct((RANK, RANK), f32),
            jax.ShapeDtypeStruct((4 * RANK, HID), bf16),
            jax.ShapeDtypeStruct((AUG, WID), bf16),
        ],
        compiler_params=pltpu.CompilerParams(vmem_limit_bytes=8 << 20),
        cost_estimate=pl.CostEstimate(flops=1 << 24, bytes_accessed=1 << 20, transcendentals=0),
        name="ortho",
    )(p, u, scaled)


def residual_kernel(first, blocks, rows, lhs, rhs, act_h, *rest):
    out, mark, held, buf, sem_in, sem_out = rest[-6:]
    mark[...] = jnp.zeros_like(mark)
    contract = (((0,), (0,)), ((), ()))

    def load(b):
        at = slice((first + b) * rows, (first + b + 1) * rows)
        return pltpu.make_async_copy(act_h.at[:, at], held.at[b, 0:EVEN, :], sem_in.at[b])

    def store(b):
        at = slice((first + b) * rows, (first + b + 1) * rows)
        return pltpu.make_async_copy(buf.at[b % 2], out.at[at, :], sem_out.at[b % 2])

    for b in range(blocks):
        load(b).start()
    for b in range(blocks):
        held[b, EVEN:AUG, :] = lhs[:, (first + b) * rows : (first + b + 1) * rows]
    for b in range(blocks):
        load(b).wait()
        if b >= 2:
            store(b - 2).wait()
        buf[b % 2] = lax.dot_general(
            held[b], rhs[...], contract, preferred_element_type=f32
        ).astype(bf16)
        store(b).start()
    for b in range(max(0, blocks - 2), blocks):
        store(b).wait()


def residual_piece(lhs, rhs, act_h, before, first, blocks, rows=512):
    anywhere, vmem = pl.BlockSpec(memory_space=pl.ANY), pl.BlockSpec(memory_space=pltpu.VMEM)
    earlier = [] if before is None else [before]
    return pl.pallas_call(
        functools.partial(residual_kernel, first, blocks, rows),
        in_specs=[vmem, vmem, anywhere] + [anywhere] * len(earlier),
        out_specs=[anywhere, vmem],
        out_shape=[jax.ShapeDtypeStruct((HID, WID), bf16), jax.ShapeDtypeStruct((RANK, LANES), f32)],
        scratch_shapes=[
            pltpu.VMEM((blocks, AUG, rows), bf16),
            pltpu.VMEM((2, rows, WID), bf16),
            pltpu.SemaphoreType.DMA((blocks,)),
            pltpu.SemaphoreType.DMA((2,)),
        ],
        input_output_aliases={3: 0} if earlier else {},
        compiler_params=pltpu.CompilerParams(vmem_limit_bytes=RES_LIMIT),
        cost_estimate=pl.CostEstimate(
            flops=PIECE_FLOPS * blocks, bytes_accessed=(2 << 20) * blocks, transcendentals=0
        ),
        name="residual",
    )(lhs, rhs, act_h, *earlier)


def finish_kernel(inverse, mine, other, q_out, *, devices):
    first = lax.axis_index("c") == 0
    half = WID // LANES // 2
    flat = jnp.concatenate(
        [jnp.where(first, mine[j], other[j]) for j in range(half)]
        + [jnp.where(first, other[j], mine[j]) for j in range(half)],
        axis=1,
    )
    q = jnp.dot(inverse[...], flat, precision=lax.Precision.HIGHEST, preferred_element_type=f32)
    q_out[...] = q * (1.0 / math.sqrt(devices))


def finish(inverse, mine, other, devices):
    return pl.pallas_call(
        functools.partial(finish_kernel, devices=devices),
        out_shape=jax.ShapeDtypeStruct((RANK, WID), f32),
        compiler_params=pltpu.CompilerParams(vmem_limit_bytes=4 << 20),
        name="finish",
    )(inverse, mine, other)


def total(v):
    terms = [v[i] for i in range(v.shape[0])]
    while len(terms) > 1:
        terms = [a + b for a, b in zip(terms[0::2], terms[1::2])]
    return terms[0]


def total_kernel(v, after, out):
    out[...] = total(v)


def total_after(v, after):
    return pl.pallas_call(
        total_kernel,
        in_specs=[pl.BlockSpec(memory_space=pltpu.VMEM)] * 2,
        out_specs=pl.BlockSpec(memory_space=pltpu.VMEM),
        out_shape=jax.ShapeDtypeStruct(v.shape[1:], f32),
        compiler_params=pltpu.CompilerParams(vmem_limit_bytes=4 << 20),
        name="total",
    )(v, after)


def swap(v):
    return lax.ppermute(v, "c", [(0, 1), (1, 0)])


def gather_all_to_all(v, axes, n):
    copies = jnp.broadcast_to(v[None], (n,) + v.shape).reshape((n * v.shape[0],) + v.shape[1:])
    return lax.all_to_all(copies, axes, 0, 0, tiled=True)


def body(pre_act, upstream, layer_scale, initial_q):
    act, act_h, scaled, p_local = front(pre_act, upstream, layer_scale.reshape(1, WID), initial_q)
    with jax.named_scope("sum_p"):
        part = total(lax.all_to_all(p_local, PLANE, 0, 0, tiled=True))
        part = total(gather_all_to_all(part[None], "z", 8))
        p_total = gather_all_to_all(part[None], PLANE, 32)
    u, keep, send = project(act, scaled, p_total)
    basis_out, inverse, lhs, rhs = ortho(p_total, u, scaled)
    early, mark = residual_piece(lhs, rhs, act_h, None, 0, SPLIT)
    residual, last_mark = residual_piece(lhs, rhs, act_h, early, SPLIT, 8 - SPLIT)
    with jax.named_scope("sum_u"):
        t = keep + swap(send)
        t = total_after(gather_all_to_all(t[None], ("x", "y"), 16).reshape(16, 4, RANK, LANES), mark)
        t = total_after(gather_all_to_all(t[None], "z", 8).reshape(8, 4, RANK, LANES), last_mark)
        other = swap(t)
    q_out = finish(inverse, t, other, 256)
    return (basis_out, q_out, residual)


def solution(mesh):
    fine = Mesh(mesh.devices.reshape(8, 4, 4, 2), ("z", "x", "y", "c"))
    split = P(("z", "x", "y", "c"), None)
    return jax.shard_map(
        body, mesh=fine, in_specs=(split, split, P(), P()), out_specs=(P(), P(), split), check_vma=False
    )
```

```python
import functools
import math

import jax
import jax.numpy as jnp
from jax import lax
from jax.experimental import pallas as pl
from jax.experimental.pallas import tpu as pltpu
from jax.sharding import Mesh
from jax.sharding import PartitionSpec as P

f32, bf16 = jnp.float32, jnp.bfloat16
ROWS, HID, WID, RANK, LANES = 588, 4096, 1024, 8, 128
EVEN, AUG = 592, 624
FRONT_LIMIT, RES_LIMIT = 52 << 20, 50 << 20
BANDS = ((0, 64), (64, 256), (256, 512), (512, ROWS))
SPANS_A = ((0, 768), (768, 1280))
SPANS_B = ((1280, 1536), (1536, 2304), (2304, 3072), (3072, 3840), (3840, 4096))
PLANE = ("x", "y", "c")


def split3(v):
    a = v.astype(bf16)
    r = v - a.astype(f32)
    b = r.astype(bf16)
    c = (r - b.astype(f32)).astype(bf16)
    return jnp.concatenate([a, b, c], axis=0)


def fold3(v):
    return v[0:RANK] + v[RANK : 2 * RANK] + v[2 * RANK : 3 * RANK]


def gelu(v):
    return 0.5 * v * (1.0 + lax.erf(v * math.sqrt(0.5)))


def front_kernel(
    slab, cols, pre_h, up_h, scale_h, q_h, act, act_h, scaled, p_out, pre, up, scale, q, reduced, sem, sem_s, sem_o
):
    def load(b):
        rows = slice(*BANDS[b])
        return pltpu.make_async_copy(pre_h.at[rows, :], pre.at[rows, :], sem.at[b])

    def store(b):
        first, last = BANDS[b]
        rows = slice(first, EVEN if last == ROWS else last)
        return pltpu.make_async_copy(act.at[rows, :], act_h.at[rows, :], sem_o.at[b])

    small = [
        pltpu.make_async_copy(q_h, q, sem_s.at[0]),
        pltpu.make_async_copy(scale_h, scale, sem_s.at[1]),
        pltpu.make_async_copy(up_h, up, sem_s.at[2]),
    ]
    load(0).start()
    for copy in small:
        copy.start()
    for b in range(1, len(BANDS)):
        load(b).start()
    act[EVEN - 16 : EVEN, :] = jnp.zeros((16, HID), bf16)
    scaled[EVEN - 16 : EVEN, :] = jnp.zeros((16, WID), bf16)
    for b, (first, last) in enumerate(BANDS):
        load(b).wait()
        for left in range(0, HID, cols):
            for r in range(first, last, slab):
                rows, at = slice(r, min(r + slab, last)), slice(left, left + cols)
                act[rows, at] = gelu(pre[rows, at].astype(f32)).astype(bf16)
        store(b).start()
    for copy in small:
        copy.wait()
    for r in range(0, ROWS, 64):
        rows = slice(r, min(r + 64, ROWS))
        scaled[rows, :] = (up[rows, :].astype(f32) * scale[...]).astype(bf16)
    r = lax.dot_general(
        split3(q[...]), scaled[...], (((1,), (1,)), ((), ())), preferred_element_type=f32
    )
    reduced[...] = split3(fold3(r))
    for left in range(0, HID, cols):
        part = fold3(jnp.dot(reduced[...], act[:, left : left + cols], preferred_element_type=f32))
        for j in range(cols // LANES):
            p_out[left // LANES + j] = part[:, j * LANES : (j + 1) * LANES]
    for b in range(len(BANDS)):
        store(b).wait()


def front(pre, up, scale, q, slab=16, cols=512):
    return pl.pallas_call(
        functools.partial(front_kernel, slab, cols),
        in_specs=[pl.BlockSpec(memory_space=pl.ANY)] * 4,
        out_specs=[pl.BlockSpec(memory_space=pltpu.VMEM if i != 1 else pl.ANY) for i in range(4)],
        out_shape=[
            pltpu.VMEM((EVEN, HID), bf16),
            pltpu.HBM((EVEN, HID), bf16),
            pltpu.VMEM((EVEN, WID), bf16),
            pltpu.VMEM((HID // LANES, RANK, LANES), f32),
        ],
        scratch_shapes=[
            pltpu.VMEM((ROWS, HID), bf16),
            pltpu.VMEM((ROWS, WID), bf16),
            pltpu.VMEM((1, WID), f32),
            pltpu.VMEM((RANK, WID), f32),
            pltpu.VMEM((3 * RANK, EVEN), bf16),
            pltpu.SemaphoreType.DMA((len(BANDS),)),
            pltpu.SemaphoreType.DMA((3,)),
            pltpu.SemaphoreType.DMA((len(BANDS),)),
        ],
        compiler_params=pltpu.CompilerParams(vmem_limit_bytes=FRONT_LIMIT),
        cost_estimate=pl.CostEstimate(flops=60 * ROWS * HID, bytes_accessed=10 << 20, transcendentals=ROWS * HID),
        name="front",
    )(pre, up, scale, q)


def project_kernel(act, scaled, p, u_out, keep, send):
    flat = jnp.concatenate([p[j] for j in range(HID // LANES)], axis=1)
    c = lax.dot_general(
        split3(flat), act[...], (((1,), (1,)), ((), ())), preferred_element_type=f32
    )
    u = fold3(jnp.dot(split3(fold3(c)), scaled[...], preferred_element_type=f32))
    core = lax.axis_index("c")
    half = WID // LANES // 2
    for j in range(half):
        low, high = (u[:, k * LANES : (k + 1) * LANES] for k in (j, half + j))
        u_out[j] = low
        u_out[half + j] = high
        keep[j] = jnp.where(core == 0, low, high)
        send[j] = jnp.where(core == 0, high, low)


def project(act, scaled, p):
    n = WID // LANES
    return pl.pallas_call(
        project_kernel,
        in_specs=[pl.BlockSpec(memory_space=pltpu.VMEM)] * 3,
        out_specs=[pl.BlockSpec(memory_space=pltpu.VMEM)] * 3,
        out_shape=[jax.ShapeDtypeStruct((k, RANK, LANES), f32) for k in (n, n // 2, n // 2)],
        compiler_params=pltpu.CompilerParams(vmem_limit_bytes=16 << 20),
        cost_estimate=pl.CostEstimate(flops=48 * ROWS * HID, bytes_accessed=6 << 20, transcendentals=0),
        name="project",
    )(act, scaled, p)


def ortho_kernel(p, u, scaled, act_h, basis, inverse, lhs, rhs, out, held, buf, sem_in, sem_out):
    finish_rows = residual_rows(SPANS_A, lhs, rhs, act_h, out, held, buf, sem_in, sem_out)
    flat = jnp.concatenate([p[j] for j in range(HID // LANES)], axis=1)
    parts = split3(flat)
    g = lax.dot_general(parts, parts, (((1,), (1,)), ((), ())), preferred_element_type=f32)
    g = fold3(g)
    gram = g[:, 0:RANK] + g[:, RANK : 2 * RANK] + g[:, 2 * RANK : 3 * RANK]
    row = lax.broadcasted_iota(jnp.int32, (RANK, RANK), 0)
    col = lax.broadcasted_iota(jnp.int32, (RANK, RANK), 1)
    inv = jnp.where(row == col, 1.0, 0.0).astype(f32)
    for j in range(RANK):
        root = lax.rsqrt(gram[j : j + 1, j : j + 1])
        gram_row, inv_row = gram[j : j + 1, :] * root, inv[j : j + 1, :] * root
        factor = jnp.where(row[:, 0:1] > j, gram[:, j : j + 1] * root, 0.0)
        gram = jnp.where(row == j, gram_row, gram - factor * gram_row)
        inv = jnp.where(row == j, inv_row, inv - factor * inv_row)
    o = jnp.dot(inv, flat, precision=lax.Precision.HIGHEST, preferred_element_type=f32)
    u_flat = jnp.concatenate([u[j] for j in range(WID // LANES)], axis=1)
    q = jnp.dot(inv, u_flat, precision=lax.Precision.HIGHEST, preferred_element_type=f32)
    basis[...] = o * math.sqrt(HID)
    inverse[...] = inv
    o_hi = (-o).astype(bf16)
    o_lo = (-o - o_hi.astype(f32)).astype(bf16)
    q_hi = q.astype(bf16)
    q_lo = (q - q_hi.astype(f32)).astype(bf16)
    lhs[...] = jnp.concatenate([o_hi, o_hi, o_lo, o_lo], axis=0)
    rhs[0:EVEN, :] = scaled[...]
    rhs[EVEN:AUG, :] = jnp.concatenate([q_hi, q_lo, q_hi, q_lo], axis=0)
    finish_rows()


def residual_rows(spans, lhs, rhs, act_h, out, held, buf, sem_in, sem_out):
    base, end = spans[0][0], spans[-1][1]

    def load(b):
        low, high = spans[b]
        return pltpu.make_async_copy(
            act_h.at[:, low:high], held.at[0:EVEN, low - base : high - base], sem_in.at[b]
        )

    def store(b):
        low, high = spans[b]
        return pltpu.make_async_copy(
            buf.at[b % 2, 0 : high - low, :], out.at[low:high, :], sem_out.at[b % 2]
        )

    for b in range(len(spans)):
        load(b).start()

    def compute():
        held[EVEN:AUG, :] = lhs[:, base:end]
        for b, (low, high) in enumerate(spans):
            load(b).wait()
            if b >= 2:
                store(b - 2).wait()
            buf[b % 2, 0 : high - low, :] = lax.dot_general(
                held[:, low - base : high - base],
                rhs[...],
                (((0,), (0,)), ((), ())),
                preferred_element_type=f32,
            ).astype(bf16)
            store(b).start()
        for b in range(max(0, len(spans) - 2), len(spans)):
            store(b).wait()

    return compute


def residual_scratch(spans):
    return [
        pltpu.VMEM((AUG, spans[-1][1] - spans[0][0]), bf16),
        pltpu.VMEM((2, max(high - low for low, high in spans), WID), bf16),
        pltpu.SemaphoreType.DMA((len(spans),)),
        pltpu.SemaphoreType.DMA((2,)),
    ]


def ortho(p, u, scaled, act_h):
    anywhere, vmem = pl.BlockSpec(memory_space=pl.ANY), pl.BlockSpec(memory_space=pltpu.VMEM)
    return pl.pallas_call(
        ortho_kernel,
        in_specs=[vmem, vmem, vmem, anywhere],
        out_specs=[vmem, vmem, vmem, vmem, anywhere],
        out_shape=[
            jax.ShapeDtypeStruct((RANK, HID), f32),
            jax.ShapeDtypeStruct((RANK, RANK), f32),
            jax.ShapeDtypeStruct((4 * RANK, HID), bf16),
            jax.ShapeDtypeStruct((AUG, WID), bf16),
            jax.ShapeDtypeStruct((HID, WID), bf16),
        ],
        scratch_shapes=residual_scratch(SPANS_A),
        compiler_params=pltpu.CompilerParams(vmem_limit_bytes=RES_LIMIT),
        cost_estimate=pl.CostEstimate(
            flops=2 * ROWS * HID * WID // 2, bytes_accessed=6 << 20, transcendentals=0
        ),
        name="ortho",
    )(p, u, scaled, act_h)


def residual_kernel(lhs, rhs, act_h, before, out, mark, held, buf, sem_in, sem_out):
    mark[...] = jnp.zeros_like(mark)
    residual_rows(SPANS_B, lhs, rhs, act_h, out, held, buf, sem_in, sem_out)()


def residual_of(lhs, rhs, act_h, before):
    anywhere, vmem = pl.BlockSpec(memory_space=pl.ANY), pl.BlockSpec(memory_space=pltpu.VMEM)
    return pl.pallas_call(
        residual_kernel,
        in_specs=[vmem, vmem, anywhere, anywhere],
        out_specs=[anywhere, vmem],
        out_shape=[jax.ShapeDtypeStruct((HID, WID), bf16), jax.ShapeDtypeStruct((RANK, LANES), f32)],
        scratch_shapes=residual_scratch(SPANS_B),
        input_output_aliases={3: 0},
        compiler_params=pltpu.CompilerParams(vmem_limit_bytes=RES_LIMIT),
        cost_estimate=pl.CostEstimate(flops=2 * ROWS * HID * WID, bytes_accessed=14 << 20, transcendentals=0),
        name="residual",
    )(lhs, rhs, act_h, before)


def finish_kernel(inverse, u, after, q_out, *, devices):
    parts = [total(u[:, core]) for core in range(2)]
    flat = jnp.concatenate([part[j] for part in parts for j in range(part.shape[0])], axis=1)
    q = jnp.dot(inverse[...], flat, precision=lax.Precision.HIGHEST, preferred_element_type=f32)
    q_out[...] = q * (1.0 / math.sqrt(devices))


def finish(inverse, u, after, devices):
    return pl.pallas_call(
        functools.partial(finish_kernel, devices=devices),
        in_specs=[pl.BlockSpec(memory_space=pltpu.VMEM)] * 3,
        out_specs=pl.BlockSpec(memory_space=pltpu.VMEM),
        out_shape=jax.ShapeDtypeStruct((RANK, WID), f32),
        compiler_params=pltpu.CompilerParams(vmem_limit_bytes=4 << 20),
        name="finish",
    )(inverse, u, after)


def total(v):
    terms = [v[i] for i in range(v.shape[0])]
    while len(terms) > 1:
        terms = [a + b for a, b in zip(terms[0::2], terms[1::2])]
    return terms[0]


def spread_kernel(v, after, out):
    whole = total(v)
    for i in range(out.shape[0]):
        out[i] = whole


def spread(v, after, n):
    return pl.pallas_call(
        spread_kernel,
        in_specs=[pl.BlockSpec(memory_space=pltpu.VMEM)] * 2,
        out_specs=pl.BlockSpec(memory_space=pltpu.VMEM),
        out_shape=pltpu.VMEM((n,) + v.shape[1:], f32),
        compiler_params=pltpu.CompilerParams(vmem_limit_bytes=4 << 20),
        name="spread",
    )(v, after)


def add_spread_kernel(a, b, out):
    whole = a[...] + b[...]
    for i in range(out.shape[0]):
        out[i] = whole


def add_spread(a, b, n):
    return pl.pallas_call(
        add_spread_kernel,
        in_specs=[pl.BlockSpec(memory_space=pltpu.VMEM)] * 2,
        out_specs=pl.BlockSpec(memory_space=pltpu.VMEM),
        out_shape=pltpu.VMEM((n,) + a.shape, f32),
        compiler_params=pltpu.CompilerParams(vmem_limit_bytes=4 << 20),
        name="add_spread",
    )(a, b)


def swap(v):
    return lax.ppermute(v, "c", [(0, 1), (1, 0)])


def gather_all_to_all(v, axes, n):
    copies = jnp.broadcast_to(v[None], (n,) + v.shape).reshape((n * v.shape[0],) + v.shape[1:])
    return lax.all_to_all(copies, axes, 0, 0, tiled=True)


def body(pre_act, upstream, layer_scale, initial_q):
    act, act_h, scaled, p_local = front(pre_act, upstream, layer_scale.reshape(1, WID), initial_q)
    with jax.named_scope("sum_p"):
        part = total(lax.all_to_all(p_local, PLANE, 0, 0, tiled=True))
        part = total(gather_all_to_all(part[None], "z", 8))
        p_total = gather_all_to_all(part[None], PLANE, 32)
    u, keep, send = project(act, scaled, p_total)
    basis_out, inverse, lhs, rhs, early = ortho(p_total, u, scaled, act_h)
    residual, mark = residual_of(lhs, rhs, act_h, early)
    with jax.named_scope("sum_u"):
        t = add_spread(keep, swap(send), 16)
        t = lax.all_to_all(t, ("x", "y"), 0, 0, tiled=True)
        t = spread(t, inverse, 16)
        t = lax.all_to_all(t, ("z", "c"), 0, 0, tiled=True)
    q_out = finish(inverse, t.reshape((8, 2) + t.shape[1:]), mark, 256)
    return (basis_out, q_out, residual)


def solution(mesh):
    fine = Mesh(mesh.devices.reshape(8, 4, 4, 2), ("z", "x", "y", "c"))
    split = P(("z", "x", "y", "c"), None)
    return jax.shard_map(
        body, mesh=fine, in_specs=(split, split, P(), P()), out_specs=(P(), P(), split), check_vma=False
    )
```

```python
import functools
import math

import jax
import jax.numpy as jnp
from jax import lax
from jax.experimental import pallas as pl
from jax.experimental.pallas import tpu as pltpu
from jax.sharding import Mesh
from jax.sharding import PartitionSpec as P

f32, bf16 = jnp.float32, jnp.bfloat16
ROWS, HID, WID, RANK, LANES = 588, 4096, 1024, 8, 128
EVEN, AUG = 592, 624
FRONT_LIMIT, RES_LIMIT = 52 << 20, 50 << 20
BANDS = ((0, 64), (64, 256), (256, 512), (512, ROWS))
SPANS_A = ((0, 768), (768, 1280))
SPANS_B = ((1280, 1536), (1536, 2304), (2304, 3072), (3072, 3840), (3840, 4096))
PLANE = ("x", "y", "c")


def split3(v):
    a = v.astype(bf16)
    r = v - a.astype(f32)
    b = r.astype(bf16)
    c = (r - b.astype(f32)).astype(bf16)
    return jnp.concatenate([a, b, c], axis=0)


def fold3(v):
    return v[0:RANK] + v[RANK : 2 * RANK] + v[2 * RANK : 3 * RANK]


def gelu(v):
    return 0.5 * v * (1.0 + lax.erf(v * math.sqrt(0.5)))


def front_kernel(
    slab, cols, pre_h, up_h, scale_h, q_h, act, act_h, scaled, p_out, pre, up, scale, q, reduced, sem, sem_s, sem_o
):
    def load(b):
        rows = slice(*BANDS[b])
        return pltpu.make_async_copy(pre_h.at[rows, :], pre.at[rows, :], sem.at[b])

    def store(b):
        first, last = BANDS[b]
        rows = slice(first, EVEN if last == ROWS else last)
        return pltpu.make_async_copy(act.at[rows, :], act_h.at[rows, :], sem_o.at[b])

    small = [
        pltpu.make_async_copy(q_h, q, sem_s.at[0]),
        pltpu.make_async_copy(scale_h, scale, sem_s.at[1]),
        pltpu.make_async_copy(up_h, up, sem_s.at[2]),
    ]
    load(0).start()
    for copy in small:
        copy.start()
    for b in range(1, len(BANDS)):
        load(b).start()
    act[EVEN - 16 : EVEN, :] = jnp.zeros((16, HID), bf16)
    scaled[EVEN - 16 : EVEN, :] = jnp.zeros((16, WID), bf16)
    for b, (first, last) in enumerate(BANDS):
        load(b).wait()
        for left in range(0, HID, cols):
            for r in range(first, last, slab):
                rows, at = slice(r, min(r + slab, last)), slice(left, left + cols)
                act[rows, at] = gelu(pre[rows, at].astype(f32)).astype(bf16)
        store(b).start()
    for copy in small:
        copy.wait()
    for r in range(0, ROWS, 64):
        rows = slice(r, min(r + 64, ROWS))
        scaled[rows, :] = (up[rows, :].astype(f32) * scale[...]).astype(bf16)
    r = lax.dot_general(
        split3(q[...]), scaled[...], (((1,), (1,)), ((), ())), preferred_element_type=f32
    )
    reduced[...] = split3(fold3(r))
    for left in range(0, HID, cols):
        part = fold3(jnp.dot(reduced[...], act[:, left : left + cols], preferred_element_type=f32))
        for j in range(cols // LANES):
            p_out[left // LANES + j] = part[:, j * LANES : (j + 1) * LANES]
    for b in range(len(BANDS)):
        store(b).wait()


def front(pre, up, scale, q, slab=16, cols=512):
    return pl.pallas_call(
        functools.partial(front_kernel, slab, cols),
        in_specs=[pl.BlockSpec(memory_space=pl.ANY)] * 4,
        out_specs=[pl.BlockSpec(memory_space=pltpu.VMEM if i != 1 else pl.ANY) for i in range(4)],
        out_shape=[
            pltpu.VMEM((EVEN, HID), bf16),
            pltpu.HBM((EVEN, HID), bf16),
            pltpu.VMEM((EVEN, WID), bf16),
            pltpu.VMEM((HID // LANES, RANK, LANES), f32),
        ],
        scratch_shapes=[
            pltpu.VMEM((ROWS, HID), bf16),
            pltpu.VMEM((ROWS, WID), bf16),
            pltpu.VMEM((1, WID), f32),
            pltpu.VMEM((RANK, WID), f32),
            pltpu.VMEM((3 * RANK, EVEN), bf16),
            pltpu.SemaphoreType.DMA((len(BANDS),)),
            pltpu.SemaphoreType.DMA((3,)),
            pltpu.SemaphoreType.DMA((len(BANDS),)),
        ],
        compiler_params=pltpu.CompilerParams(vmem_limit_bytes=FRONT_LIMIT),
        cost_estimate=pl.CostEstimate(flops=60 * ROWS * HID, bytes_accessed=10 << 20, transcendentals=ROWS * HID),
        name="front",
    )(pre, up, scale, q)


def project_kernel(act, scaled, p, u_out, keep, send):
    flat = jnp.concatenate([p[j] for j in range(HID // LANES)], axis=1)
    c = lax.dot_general(
        split3(flat), act[...], (((1,), (1,)), ((), ())), preferred_element_type=f32
    )
    u = fold3(jnp.dot(split3(fold3(c)), scaled[...], preferred_element_type=f32))
    core = lax.axis_index("c")
    half = WID // LANES // 2
    for j in range(half):
        low, high = (u[:, k * LANES : (k + 1) * LANES] for k in (j, half + j))
        u_out[j] = low
        u_out[half + j] = high
        keep[j] = jnp.where(core == 0, low, high)
        send[j] = jnp.where(core == 0, high, low)


def project(act, scaled, p):
    n = WID // LANES
    return pl.pallas_call(
        project_kernel,
        in_specs=[pl.BlockSpec(memory_space=pltpu.VMEM)] * 3,
        out_specs=[pl.BlockSpec(memory_space=pltpu.VMEM)] * 3,
        out_shape=[jax.ShapeDtypeStruct((k, RANK, LANES), f32) for k in (n, n // 2, n // 2)],
        compiler_params=pltpu.CompilerParams(vmem_limit_bytes=16 << 20),
        cost_estimate=pl.CostEstimate(flops=48 * ROWS * HID, bytes_accessed=6 << 20, transcendentals=0),
        name="project",
    )(act, scaled, p)


def ortho_kernel(p, u, scaled, act_h, basis, inverse, lhs, rhs, out, held, buf, sem_in, sem_out):
    finish_rows = residual_rows(SPANS_A, lhs, rhs, act_h, out, held, buf, sem_in, sem_out)
    flat = jnp.concatenate([p[j] for j in range(HID // LANES)], axis=1)
    parts = split3(flat)
    g = lax.dot_general(parts, parts, (((1,), (1,)), ((), ())), preferred_element_type=f32)
    g = fold3(g)
    gram = g[:, 0:RANK] + g[:, RANK : 2 * RANK] + g[:, 2 * RANK : 3 * RANK]
    row = lax.broadcasted_iota(jnp.int32, (RANK, RANK), 0)
    col = lax.broadcasted_iota(jnp.int32, (RANK, RANK), 1)
    inv = jnp.where(row == col, 1.0, 0.0).astype(f32)
    for j in range(RANK):
        root = lax.rsqrt(gram[j : j + 1, j : j + 1])
        gram_row, inv_row = gram[j : j + 1, :] * root, inv[j : j + 1, :] * root
        factor = jnp.where(row[:, 0:1] > j, gram[:, j : j + 1] * root, 0.0)
        gram = jnp.where(row == j, gram_row, gram - factor * gram_row)
        inv = jnp.where(row == j, inv_row, inv - factor * inv_row)
    o = jnp.dot(inv, flat, precision=lax.Precision.HIGHEST, preferred_element_type=f32)
    u_flat = jnp.concatenate([u[j] for j in range(WID // LANES)], axis=1)
    q = jnp.dot(inv, u_flat, precision=lax.Precision.HIGHEST, preferred_element_type=f32)
    basis[...] = o * math.sqrt(HID)
    inverse[...] = inv
    o_hi = (-o).astype(bf16)
    o_lo = (-o - o_hi.astype(f32)).astype(bf16)
    q_hi = q.astype(bf16)
    q_lo = (q - q_hi.astype(f32)).astype(bf16)
    lhs[...] = jnp.concatenate([o_hi, o_hi, o_lo, o_lo], axis=0)
    rhs[0:EVEN, :] = scaled[...]
    rhs[EVEN:AUG, :] = jnp.concatenate([q_hi, q_lo, q_hi, q_lo], axis=0)
    finish_rows()


def residual_rows(spans, lhs, rhs, act_h, out, held, buf, sem_in, sem_out):
    base, end = spans[0][0], spans[-1][1]

    def load(b):
        low, high = spans[b]
        return pltpu.make_async_copy(
            act_h.at[:, low:high], held.at[0:EVEN, low - base : high - base], sem_in.at[b]
        )

    def store(b):
        low, high = spans[b]
        return pltpu.make_async_copy(
            buf.at[b % 2, 0 : high - low, :], out.at[low:high, :], sem_out.at[b % 2]
        )

    for b in range(len(spans)):
        load(b).start()

    def compute():
        held[EVEN:AUG, :] = lhs[:, base:end]
        for b, (low, high) in enumerate(spans):
            load(b).wait()
            if b >= 2:
                store(b - 2).wait()
            buf[b % 2, 0 : high - low, :] = lax.dot_general(
                held[:, low - base : high - base],
                rhs[...],
                (((0,), (0,)), ((), ())),
                preferred_element_type=f32,
            ).astype(bf16)
            store(b).start()
        for b in range(max(0, len(spans) - 2), len(spans)):
            store(b).wait()

    return compute


def residual_scratch(spans):
    return [
        pltpu.VMEM((AUG, spans[-1][1] - spans[0][0]), bf16),
        pltpu.VMEM((2, max(high - low for low, high in spans), WID), bf16),
        pltpu.SemaphoreType.DMA((len(spans),)),
        pltpu.SemaphoreType.DMA((2,)),
    ]


def ortho(p, u, scaled, act_h):
    anywhere, vmem = pl.BlockSpec(memory_space=pl.ANY), pl.BlockSpec(memory_space=pltpu.VMEM)
    return pl.pallas_call(
        ortho_kernel,
        in_specs=[vmem, vmem, vmem, anywhere],
        out_specs=[vmem, vmem, vmem, vmem, anywhere],
        out_shape=[
            jax.ShapeDtypeStruct((RANK, HID), f32),
            jax.ShapeDtypeStruct((RANK, RANK), f32),
            jax.ShapeDtypeStruct((4 * RANK, HID), bf16),
            jax.ShapeDtypeStruct((AUG, WID), bf16),
            jax.ShapeDtypeStruct((HID, WID), bf16),
        ],
        scratch_shapes=residual_scratch(SPANS_A),
        compiler_params=pltpu.CompilerParams(vmem_limit_bytes=RES_LIMIT),
        cost_estimate=pl.CostEstimate(
            flops=2 * ROWS * HID * WID // 2, bytes_accessed=6 << 20, transcendentals=0
        ),
        name="ortho",
    )(p, u, scaled, act_h)


def residual_kernel(lhs, rhs, act_h, before, out, mark, held, buf, sem_in, sem_out):
    mark[...] = jnp.zeros_like(mark)
    residual_rows(SPANS_B, lhs, rhs, act_h, out, held, buf, sem_in, sem_out)()


def residual_of(lhs, rhs, act_h, before):
    anywhere, vmem = pl.BlockSpec(memory_space=pl.ANY), pl.BlockSpec(memory_space=pltpu.VMEM)
    return pl.pallas_call(
        residual_kernel,
        in_specs=[vmem, vmem, anywhere, anywhere],
        out_specs=[anywhere, vmem],
        out_shape=[jax.ShapeDtypeStruct((HID, WID), bf16), jax.ShapeDtypeStruct((RANK, LANES), f32)],
        scratch_shapes=residual_scratch(SPANS_B),
        input_output_aliases={3: 0},
        compiler_params=pltpu.CompilerParams(vmem_limit_bytes=RES_LIMIT),
        cost_estimate=pl.CostEstimate(flops=2 * ROWS * HID * WID, bytes_accessed=14 << 20, transcendentals=0),
        name="residual",
    )(lhs, rhs, act_h, before)


def finish_kernel(inverse, mine, other, q_out, *, devices):
    first = lax.axis_index("c") == 0
    half = WID // LANES // 2
    flat = jnp.concatenate(
        [jnp.where(first, mine[j], other[j]) for j in range(half)]
        + [jnp.where(first, other[j], mine[j]) for j in range(half)],
        axis=1,
    )
    q = jnp.dot(inverse[...], flat, precision=lax.Precision.HIGHEST, preferred_element_type=f32)
    q_out[...] = q * (1.0 / math.sqrt(devices))


def finish(inverse, mine, other, devices):
    return pl.pallas_call(
        functools.partial(finish_kernel, devices=devices),
        in_specs=[pl.BlockSpec(memory_space=pltpu.VMEM)] * 3,
        out_specs=pl.BlockSpec(memory_space=pltpu.VMEM),
        out_shape=jax.ShapeDtypeStruct((RANK, WID), f32),
        compiler_params=pltpu.CompilerParams(vmem_limit_bytes=4 << 20),
        name="finish",
    )(inverse, mine, other)


def total(v):
    terms = [v[i] for i in range(v.shape[0])]
    while len(terms) > 1:
        terms = [a + b for a, b in zip(terms[0::2], terms[1::2])]
    return terms[0]


def total_kernel(v, after, out):
    out[...] = total(v)


def total_after(v, after):
    return pl.pallas_call(
        total_kernel,
        in_specs=[pl.BlockSpec(memory_space=pltpu.VMEM)] * 2,
        out_specs=pl.BlockSpec(memory_space=pltpu.VMEM),
        out_shape=jax.ShapeDtypeStruct(v.shape[1:], f32),
        compiler_params=pltpu.CompilerParams(vmem_limit_bytes=4 << 20),
        name="total",
    )(v, after)


def spread_kernel(v, after, out):
    whole = total(v)
    for i in range(out.shape[0]):
        out[i] = whole


def spread(v, after, n):
    return pl.pallas_call(
        spread_kernel,
        in_specs=[pl.BlockSpec(memory_space=pltpu.VMEM)] * 2,
        out_specs=pl.BlockSpec(memory_space=pltpu.VMEM),
        out_shape=pltpu.VMEM((n,) + v.shape[1:], f32),
        compiler_params=pltpu.CompilerParams(vmem_limit_bytes=4 << 20),
        name="spread",
    )(v, after)


def add_spread_kernel(a, b, out):
    whole = a[...] + b[...]
    for i in range(out.shape[0]):
        out[i] = whole


def add_spread(a, b, n):
    return pl.pallas_call(
        add_spread_kernel,
        in_specs=[pl.BlockSpec(memory_space=pltpu.VMEM)] * 2,
        out_specs=pl.BlockSpec(memory_space=pltpu.VMEM),
        out_shape=pltpu.VMEM((n,) + a.shape, f32),
        compiler_params=pltpu.CompilerParams(vmem_limit_bytes=4 << 20),
        name="add_spread",
    )(a, b)


def swap(v):
    return lax.ppermute(v, "c", [(0, 1), (1, 0)])


def gather_all_to_all(v, axes, n):
    copies = jnp.broadcast_to(v[None], (n,) + v.shape).reshape((n * v.shape[0],) + v.shape[1:])
    return lax.all_to_all(copies, axes, 0, 0, tiled=True)


def body(pre_act, upstream, layer_scale, initial_q):
    act, act_h, scaled, p_local = front(pre_act, upstream, layer_scale.reshape(1, WID), initial_q)
    with jax.named_scope("sum_p"):
        part = total(lax.all_to_all(p_local, PLANE, 0, 0, tiled=True))
        part = total(gather_all_to_all(part[None], "z", 8))
        p_total = gather_all_to_all(part[None], PLANE, 32)
    u, keep, send = project(act, scaled, p_total)
    basis_out, inverse, lhs, rhs, early = ortho(p_total, u, scaled, act_h)
    residual, mark = residual_of(lhs, rhs, act_h, early)
    with jax.named_scope("sum_u"):
        t = add_spread(keep, swap(send), 16)
        t = lax.all_to_all(t, ("x", "y"), 0, 0, tiled=True)
        t = spread(t, inverse, 8)
        mine = total_after(lax.all_to_all(t, "z", 0, 0, tiled=True), mark)
        other = swap(mine)
    q_out = finish(inverse, mine, other, 256)
    return (basis_out, q_out, residual)


def solution(mesh):
    fine = Mesh(mesh.devices.reshape(8, 4, 4, 2), ("z", "x", "y", "c"))
    split = P(("z", "x", "y", "c"), None)
    return jax.shard_map(
        body, mesh=fine, in_specs=(split, split, P(), P()), out_specs=(P(), P(), split), check_vma=False
    )
```

```python
import functools
import math

import jax
import jax.numpy as jnp
from jax import lax
from jax.experimental import pallas as pl
from jax.experimental.pallas import tpu as pltpu
from jax.sharding import Mesh
from jax.sharding import PartitionSpec as P

f32, bf16 = jnp.float32, jnp.bfloat16
ROWS, HID, WID, RANK, LANES = 588, 4096, 1024, 8, 128
EVEN, AUG = 592, 624
FRONT_LIMIT, RES_LIMIT = 52 << 20, 50 << 20
BANDS = ((0, 64), (64, 256), (256, 512), (512, ROWS))
SPANS_A = ((0, 768), (768, 1536), (1536, 2048))
SPANS_B = ((2048, 2304), (2304, 3072), (3072, 3840), (3840, 4096))
PLANE = ("x", "y", "c")


def split3(v):
    a = v.astype(bf16)
    r = v - a.astype(f32)
    b = r.astype(bf16)
    c = (r - b.astype(f32)).astype(bf16)
    return jnp.concatenate([a, b, c], axis=0)


def fold3(v):
    return v[0:RANK] + v[RANK : 2 * RANK] + v[2 * RANK : 3 * RANK]


def gelu(v):
    return 0.5 * v * (1.0 + lax.erf(v * math.sqrt(0.5)))


def front_kernel(
    slab, cols, pre_h, up_h, scale_h, q_h, act, act_h, scaled, p_out, pre, up, scale, q, reduced, sem, sem_s, sem_o
):
    def load(b):
        rows = slice(*BANDS[b])
        return pltpu.make_async_copy(pre_h.at[rows, :], pre.at[rows, :], sem.at[b])

    def store(b):
        first, last = BANDS[b]
        rows = slice(first, EVEN if last == ROWS else last)
        return pltpu.make_async_copy(act.at[rows, :], act_h.at[rows, :], sem_o.at[b])

    small = [
        pltpu.make_async_copy(q_h, q, sem_s.at[0]),
        pltpu.make_async_copy(scale_h, scale, sem_s.at[1]),
        pltpu.make_async_copy(up_h, up, sem_s.at[2]),
    ]
    load(0).start()
    for copy in small:
        copy.start()
    for b in range(1, len(BANDS)):
        load(b).start()
    act[EVEN - 16 : EVEN, :] = jnp.zeros((16, HID), bf16)
    scaled[EVEN - 16 : EVEN, :] = jnp.zeros((16, WID), bf16)
    for b, (first, last) in enumerate(BANDS):
        load(b).wait()
        for left in range(0, HID, cols):
            for r in range(first, last, slab):
                rows, at = slice(r, min(r + slab, last)), slice(left, left + cols)
                act[rows, at] = gelu(pre[rows, at].astype(f32)).astype(bf16)
        store(b).start()
    for copy in small:
        copy.wait()
    for r in range(0, ROWS, 64):
        rows = slice(r, min(r + 64, ROWS))
        scaled[rows, :] = (up[rows, :].astype(f32) * scale[...]).astype(bf16)
    r = lax.dot_general(
        split3(q[...]), scaled[...], (((1,), (1,)), ((), ())), preferred_element_type=f32
    )
    reduced[...] = split3(fold3(r))
    for left in range(0, HID, cols):
        part = fold3(jnp.dot(reduced[...], act[:, left : left + cols], preferred_element_type=f32))
        for j in range(cols // LANES):
            p_out[left // LANES + j] = part[:, j * LANES : (j + 1) * LANES]
    for b in range(len(BANDS)):
        store(b).wait()


def front(pre, up, scale, q, slab=16, cols=512):
    return pl.pallas_call(
        functools.partial(front_kernel, slab, cols),
        in_specs=[pl.BlockSpec(memory_space=pl.ANY)] * 4,
        out_specs=[pl.BlockSpec(memory_space=pltpu.VMEM if i != 1 else pl.ANY) for i in range(4)],
        out_shape=[
            pltpu.VMEM((EVEN, HID), bf16),
            pltpu.HBM((EVEN, HID), bf16),
            pltpu.VMEM((EVEN, WID), bf16),
            pltpu.VMEM((HID // LANES, RANK, LANES), f32),
        ],
        scratch_shapes=[
            pltpu.VMEM((ROWS, HID), bf16),
            pltpu.VMEM((ROWS, WID), bf16),
            pltpu.VMEM((1, WID), f32),
            pltpu.VMEM((RANK, WID), f32),
            pltpu.VMEM((3 * RANK, EVEN), bf16),
            pltpu.SemaphoreType.DMA((len(BANDS),)),
            pltpu.SemaphoreType.DMA((3,)),
            pltpu.SemaphoreType.DMA((len(BANDS),)),
        ],
        compiler_params=pltpu.CompilerParams(vmem_limit_bytes=FRONT_LIMIT),
        cost_estimate=pl.CostEstimate(flops=60 * ROWS * HID, bytes_accessed=10 << 20, transcendentals=ROWS * HID),
        name="front",
    )(pre, up, scale, q)


def project_kernel(act, scaled, p, u_out, keep, send):
    flat = jnp.concatenate([p[j] for j in range(HID // LANES)], axis=1)
    c = lax.dot_general(
        split3(flat), act[...], (((1,), (1,)), ((), ())), preferred_element_type=f32
    )
    u = fold3(jnp.dot(split3(fold3(c)), scaled[...], preferred_element_type=f32))
    core = lax.axis_index("c")
    half = WID // LANES // 2
    for j in range(half):
        low, high = (u[:, k * LANES : (k + 1) * LANES] for k in (j, half + j))
        u_out[j] = low
        u_out[half + j] = high
        keep[j] = jnp.where(core == 0, low, high)
        send[j] = jnp.where(core == 0, high, low)


def project(act, scaled, p):
    n = WID // LANES
    return pl.pallas_call(
        project_kernel,
        in_specs=[pl.BlockSpec(memory_space=pltpu.VMEM)] * 3,
        out_specs=[pl.BlockSpec(memory_space=pltpu.VMEM)] * 3,
        out_shape=[jax.ShapeDtypeStruct((k, RANK, LANES), f32) for k in (n, n // 2, n // 2)],
        compiler_params=pltpu.CompilerParams(vmem_limit_bytes=16 << 20),
        cost_estimate=pl.CostEstimate(flops=48 * ROWS * HID, bytes_accessed=6 << 20, transcendentals=0),
        name="project",
    )(act, scaled, p)


def ortho_kernel(p, u, scaled, act_h, basis, inverse, lhs, rhs, out, held, buf, sem_in, sem_out):
    finish_rows = residual_rows(SPANS_A, lhs, rhs, act_h, out, held, buf, sem_in, sem_out)
    flat = jnp.concatenate([p[j] for j in range(HID // LANES)], axis=1)
    parts = split3(flat)
    g = lax.dot_general(parts, parts, (((1,), (1,)), ((), ())), preferred_element_type=f32)
    g = fold3(g)
    gram = g[:, 0:RANK] + g[:, RANK : 2 * RANK] + g[:, 2 * RANK : 3 * RANK]
    row = lax.broadcasted_iota(jnp.int32, (RANK, RANK), 0)
    col = lax.broadcasted_iota(jnp.int32, (RANK, RANK), 1)
    inv = jnp.where(row == col, 1.0, 0.0).astype(f32)
    for j in range(RANK):
        root = lax.rsqrt(gram[j : j + 1, j : j + 1])
        gram_row, inv_row = gram[j : j + 1, :] * root, inv[j : j + 1, :] * root
        factor = jnp.where(row[:, 0:1] > j, gram[:, j : j + 1] * root, 0.0)
        gram = jnp.where(row == j, gram_row, gram - factor * gram_row)
        inv = jnp.where(row == j, inv_row, inv - factor * inv_row)
    o = jnp.dot(inv, flat, precision=lax.Precision.HIGHEST, preferred_element_type=f32)
    u_flat = jnp.concatenate([u[j] for j in range(WID // LANES)], axis=1)
    q = jnp.dot(inv, u_flat, precision=lax.Precision.HIGHEST, preferred_element_type=f32)
    basis[...] = o * math.sqrt(HID)
    inverse[...] = inv
    o_hi = (-o).astype(bf16)
    o_lo = (-o - o_hi.astype(f32)).astype(bf16)
    q_hi = q.astype(bf16)
    q_lo = (q - q_hi.astype(f32)).astype(bf16)
    lhs[...] = jnp.concatenate([o_hi, o_hi, o_lo, o_lo], axis=0)
    rhs[0:EVEN, :] = scaled[...]
    rhs[EVEN:AUG, :] = jnp.concatenate([q_hi, q_lo, q_hi, q_lo], axis=0)
    finish_rows()


def residual_rows(spans, lhs, rhs, act_h, out, held, buf, sem_in, sem_out):
    base, end = spans[0][0], spans[-1][1]

    def load(b):
        low, high = spans[b]
        return pltpu.make_async_copy(
            act_h.at[:, low:high], held.at[0:EVEN, low - base : high - base], sem_in.at[b]
        )

    def store(b):
        low, high = spans[b]
        return pltpu.make_async_copy(
            buf.at[b % 2, 0 : high - low, :], out.at[low:high, :], sem_out.at[b % 2]
        )

    for b in range(len(spans)):
        load(b).start()

    def compute():
        held[EVEN:AUG, :] = lhs[:, base:end]
        for b, (low, high) in enumerate(spans):
            load(b).wait()
            if b >= 2:
                store(b - 2).wait()
            buf[b % 2, 0 : high - low, :] = lax.dot_general(
                held[:, low - base : high - base],
                rhs[...],
                (((0,), (0,)), ((), ())),
                preferred_element_type=f32,
            ).astype(bf16)
            store(b).start()
        for b in range(max(0, len(spans) - 2), len(spans)):
            store(b).wait()

    return compute


def residual_scratch(spans):
    return [
        pltpu.VMEM((AUG, spans[-1][1] - spans[0][0]), bf16),
        pltpu.VMEM((2, max(high - low for low, high in spans), WID), bf16),
        pltpu.SemaphoreType.DMA((len(spans),)),
        pltpu.SemaphoreType.DMA((2,)),
    ]


def ortho(p, u, scaled, act_h):
    anywhere, vmem = pl.BlockSpec(memory_space=pl.ANY), pl.BlockSpec(memory_space=pltpu.VMEM)
    return pl.pallas_call(
        ortho_kernel,
        in_specs=[vmem, vmem, vmem, anywhere],
        out_specs=[vmem, vmem, vmem, vmem, anywhere],
        out_shape=[
            jax.ShapeDtypeStruct((RANK, HID), f32),
            jax.ShapeDtypeStruct((RANK, RANK), f32),
            jax.ShapeDtypeStruct((4 * RANK, HID), bf16),
            jax.ShapeDtypeStruct((AUG, WID), bf16),
            jax.ShapeDtypeStruct((HID, WID), bf16),
        ],
        scratch_shapes=residual_scratch(SPANS_A),
        compiler_params=pltpu.CompilerParams(vmem_limit_bytes=RES_LIMIT),
        cost_estimate=pl.CostEstimate(
            flops=2 * ROWS * HID * WID // 2, bytes_accessed=6 << 20, transcendentals=0
        ),
        name="ortho",
    )(p, u, scaled, act_h)


def residual_kernel(lhs, rhs, act_h, before, out, mark, held, buf, sem_in, sem_out):
    mark[...] = jnp.zeros_like(mark)
    residual_rows(SPANS_B, lhs, rhs, act_h, out, held, buf, sem_in, sem_out)()


def residual_of(lhs, rhs, act_h, before):
    anywhere, vmem = pl.BlockSpec(memory_space=pl.ANY), pl.BlockSpec(memory_space=pltpu.VMEM)
    return pl.pallas_call(
        residual_kernel,
        in_specs=[vmem, vmem, anywhere, anywhere],
        out_specs=[anywhere, vmem],
        out_shape=[jax.ShapeDtypeStruct((HID, WID), bf16), jax.ShapeDtypeStruct((RANK, LANES), f32)],
        scratch_shapes=residual_scratch(SPANS_B),
        input_output_aliases={3: 0},
        compiler_params=pltpu.CompilerParams(vmem_limit_bytes=RES_LIMIT),
        cost_estimate=pl.CostEstimate(flops=2 * ROWS * HID * WID, bytes_accessed=14 << 20, transcendentals=0),
        name="residual",
    )(lhs, rhs, act_h, before)


def finish_kernel(inverse, mine, other, q_out, *, devices):
    first = lax.axis_index("c") == 0
    half = WID // LANES // 2
    flat = jnp.concatenate(
        [jnp.where(first, mine[j], other[j]) for j in range(half)]
        + [jnp.where(first, other[j], mine[j]) for j in range(half)],
        axis=1,
    )
    q = jnp.dot(inverse[...], flat, precision=lax.Precision.HIGHEST, preferred_element_type=f32)
    q_out[...] = q * (1.0 / math.sqrt(devices))


def finish(inverse, mine, other, devices):
    return pl.pallas_call(
        functools.partial(finish_kernel, devices=devices),
        in_specs=[pl.BlockSpec(memory_space=pltpu.VMEM)] * 3,
        out_specs=pl.BlockSpec(memory_space=pltpu.VMEM),
        out_shape=jax.ShapeDtypeStruct((RANK, WID), f32),
        compiler_params=pltpu.CompilerParams(vmem_limit_bytes=4 << 20),
        name="finish",
    )(inverse, mine, other)


def total(v):
    terms = [v[i] for i in range(v.shape[0])]
    while len(terms) > 1:
        terms = [a + b for a, b in zip(terms[0::2], terms[1::2])]
    return terms[0]


def total_kernel(v, after, out):
    out[...] = total(v)


def total_after(v, after):
    return pl.pallas_call(
        total_kernel,
        in_specs=[pl.BlockSpec(memory_space=pltpu.VMEM)] * 2,
        out_specs=pl.BlockSpec(memory_space=pltpu.VMEM),
        out_shape=jax.ShapeDtypeStruct(v.shape[1:], f32),
        compiler_params=pltpu.CompilerParams(vmem_limit_bytes=4 << 20),
        name="total",
    )(v, after)


def spread_kernel(v, after, out):
    whole = total(v)
    for i in range(out.shape[0]):
        out[i] = whole


def spread(v, after, n):
    return pl.pallas_call(
        spread_kernel,
        in_specs=[pl.BlockSpec(memory_space=pltpu.VMEM)] * 2,
        out_specs=pl.BlockSpec(memory_space=pltpu.VMEM),
        out_shape=pltpu.VMEM((n,) + v.shape[1:], f32),
        compiler_params=pltpu.CompilerParams(vmem_limit_bytes=4 << 20),
        name="spread",
    )(v, after)


def add_spread_kernel(a, b, out):
    whole = a[...] + b[...]
    for i in range(out.shape[0]):
        out[i] = whole


def add_spread(a, b, n):
    return pl.pallas_call(
        add_spread_kernel,
        in_specs=[pl.BlockSpec(memory_space=pltpu.VMEM)] * 2,
        out_specs=pl.BlockSpec(memory_space=pltpu.VMEM),
        out_shape=pltpu.VMEM((n,) + a.shape, f32),
        compiler_params=pltpu.CompilerParams(vmem_limit_bytes=4 << 20),
        name="add_spread",
    )(a, b)


def swap(v):
    return lax.ppermute(v, "c", [(0, 1), (1, 0)])


def gather_all_to_all(v, axes, n):
    copies = jnp.broadcast_to(v[None], (n,) + v.shape).reshape((n * v.shape[0],) + v.shape[1:])
    return lax.all_to_all(copies, axes, 0, 0, tiled=True)


def body(pre_act, upstream, layer_scale, initial_q):
    act, act_h, scaled, p_local = front(pre_act, upstream, layer_scale.reshape(1, WID), initial_q)
    with jax.named_scope("sum_p"):
        part = total(lax.all_to_all(p_local, PLANE, 0, 0, tiled=True))
        part = total(gather_all_to_all(part[None], "z", 8))
        p_total = gather_all_to_all(part[None], PLANE, 32)
    u, keep, send = project(act, scaled, p_total)
    basis_out, inverse, lhs, rhs, early = ortho(p_total, u, scaled, act_h)
    residual, mark = residual_of(lhs, rhs, act_h, early)
    with jax.named_scope("sum_u"):
        t = add_spread(keep, swap(send), 8)
        t = lax.all_to_all(t, "z", 0, 0, tiled=True)
        t = spread(t, inverse, 16)
        mine = total_after(lax.all_to_all(t, ("x", "y"), 0, 0, tiled=True), mark)
        other = swap(mine)
    q_out = finish(inverse, mine, other, 256)
    return (basis_out, q_out, residual)


def solution(mesh):
    fine = Mesh(mesh.devices.reshape(8, 4, 4, 2), ("z", "x", "y", "c"))
    split = P(("z", "x", "y", "c"), None)
    return jax.shard_map(
        body, mesh=fine, in_specs=(split, split, P(), P()), out_specs=(P(), P(), split), check_vma=False
    )
```

```python
import functools
import math

import jax
import jax.numpy as jnp
from jax import lax
from jax.experimental import pallas as pl
from jax.experimental.pallas import tpu as pltpu
from jax.sharding import Mesh
from jax.sharding import PartitionSpec as P

f32, bf16 = jnp.float32, jnp.bfloat16
ROWS, HID, WID, RANK, LANES = 588, 4096, 1024, 8, 128
EVEN, AUG = 592, 624
FRONT_LIMIT, RES_LIMIT = 52 << 20, 50 << 20
BANDS = ((0, 64), (64, 256), (256, 512), (512, ROWS))
SPANS_A = ((0, 768), (768, 1280))
SPANS_B = ((1280, 1536), (1536, 2304), (2304, 3072), (3072, 3840), (3840, 4096))
PLANE = ("x", "y", "c")


def split3(v):
    a = v.astype(bf16)
    r = v - a.astype(f32)
    b = r.astype(bf16)
    c = (r - b.astype(f32)).astype(bf16)
    return jnp.concatenate([a, b, c], axis=0)


def fold3(v):
    return v[0:RANK] + v[RANK : 2 * RANK] + v[2 * RANK : 3 * RANK]


def gelu(v):
    return 0.5 * v * (1.0 + lax.erf(v * math.sqrt(0.5)))


def front_kernel(
    slab, cols, pre_h, up_h, scale_h, q_h, act, act_h, scaled, p_out, pre, up, scale, q, reduced, sem, sem_s, sem_o
):
    def load(b):
        rows = slice(*BANDS[b])
        return pltpu.make_async_copy(pre_h.at[rows, :], pre.at[rows, :], sem.at[b])

    def store(b):
        first, last = BANDS[b]
        rows = slice(first, EVEN if last == ROWS else last)
        return pltpu.make_async_copy(act.at[rows, :], act_h.at[rows, :], sem_o.at[b])

    small = [
        pltpu.make_async_copy(q_h, q, sem_s.at[0]),
        pltpu.make_async_copy(scale_h, scale, sem_s.at[1]),
        pltpu.make_async_copy(up_h, up, sem_s.at[2]),
    ]
    load(0).start()
    for copy in small:
        copy.start()
    for b in range(1, len(BANDS)):
        load(b).start()
    act[EVEN - 16 : EVEN, :] = jnp.zeros((16, HID), bf16)
    scaled[EVEN - 16 : EVEN, :] = jnp.zeros((16, WID), bf16)
    for b, (first, last) in enumerate(BANDS):
        load(b).wait()
        for left in range(0, HID, cols):
            for r in range(first, last, slab):
                rows, at = slice(r, min(r + slab, last)), slice(left, left + cols)
                act[rows, at] = gelu(pre[rows, at].astype(f32)).astype(bf16)
        store(b).start()
    for copy in small:
        copy.wait()
    for r in range(0, ROWS, 64):
        rows = slice(r, min(r + 64, ROWS))
        scaled[rows, :] = (up[rows, :].astype(f32) * scale[...]).astype(bf16)
    r = lax.dot_general(
        split3(q[...]), scaled[...], (((1,), (1,)), ((), ())), preferred_element_type=f32
    )
    reduced[...] = split3(fold3(r))
    for left in range(0, HID, cols):
        part = fold3(jnp.dot(reduced[...], act[:, left : left + cols], preferred_element_type=f32))
        for j in range(cols // LANES):
            p_out[left // LANES + j] = part[:, j * LANES : (j + 1) * LANES]
    for b in range(len(BANDS)):
        store(b).wait()


def front(pre, up, scale, q, slab=16, cols=512):
    return pl.pallas_call(
        functools.partial(front_kernel, slab, cols),
        in_specs=[pl.BlockSpec(memory_space=pl.ANY)] * 4,
        out_specs=[pl.BlockSpec(memory_space=pltpu.VMEM if i != 1 else pl.ANY) for i in range(4)],
        out_shape=[
            pltpu.VMEM((EVEN, HID), bf16),
            pltpu.HBM((EVEN, HID), bf16),
            pltpu.VMEM((EVEN, WID), bf16),
            pltpu.VMEM((HID // LANES, RANK, LANES), f32),
        ],
        scratch_shapes=[
            pltpu.VMEM((ROWS, HID), bf16),
            pltpu.VMEM((ROWS, WID), bf16),
            pltpu.VMEM((1, WID), f32),
            pltpu.VMEM((RANK, WID), f32),
            pltpu.VMEM((3 * RANK, EVEN), bf16),
            pltpu.SemaphoreType.DMA((len(BANDS),)),
            pltpu.SemaphoreType.DMA((3,)),
            pltpu.SemaphoreType.DMA((len(BANDS),)),
        ],
        compiler_params=pltpu.CompilerParams(vmem_limit_bytes=FRONT_LIMIT),
        cost_estimate=pl.CostEstimate(flops=60 * ROWS * HID, bytes_accessed=10 << 20, transcendentals=ROWS * HID),
        name="front",
    )(pre, up, scale, q)


def project_kernel(act, scaled, p, u_out, keep, send):
    flat = jnp.concatenate([p[j] for j in range(HID // LANES)], axis=1)
    c = lax.dot_general(
        act[...], split3(flat), (((1,), (1,)), ((), ())), preferred_element_type=f32
    ).T
    u = fold3(jnp.dot(split3(fold3(c)), scaled[...], preferred_element_type=f32))
    core = lax.axis_index("c")
    half = WID // LANES // 2
    for j in range(half):
        low, high = (u[:, k * LANES : (k + 1) * LANES] for k in (j, half + j))
        u_out[j] = low
        u_out[half + j] = high
        keep[j] = jnp.where(core == 0, low, high)
        send[j] = jnp.where(core == 0, high, low)


def project(act, scaled, p):
    n = WID // LANES
    return pl.pallas_call(
        project_kernel,
        in_specs=[pl.BlockSpec(memory_space=pltpu.VMEM)] * 3,
        out_specs=[pl.BlockSpec(memory_space=pltpu.VMEM)] * 3,
        out_shape=[jax.ShapeDtypeStruct((k, RANK, LANES), f32) for k in (n, n // 2, n // 2)],
        compiler_params=pltpu.CompilerParams(vmem_limit_bytes=16 << 20),
        cost_estimate=pl.CostEstimate(flops=48 * ROWS * HID, bytes_accessed=6 << 20, transcendentals=0),
        name="project",
    )(act, scaled, p)


def ortho_kernel(p, u, scaled, act_h, basis, inverse, lhs, rhs, out, held, buf, sem_in, sem_out):
    finish_rows = residual_rows(SPANS_A, lhs, rhs, act_h, out, held, buf, sem_in, sem_out)
    flat = jnp.concatenate([p[j] for j in range(HID // LANES)], axis=1)
    parts = split3(flat)
    g = lax.dot_general(parts, parts, (((1,), (1,)), ((), ())), preferred_element_type=f32)
    g = fold3(g)
    gram = g[:, 0:RANK] + g[:, RANK : 2 * RANK] + g[:, 2 * RANK : 3 * RANK]
    row = lax.broadcasted_iota(jnp.int32, (RANK, RANK), 0)
    col = lax.broadcasted_iota(jnp.int32, (RANK, RANK), 1)
    inv = jnp.where(row == col, 1.0, 0.0).astype(f32)
    for j in range(RANK):
        root = lax.rsqrt(gram[j : j + 1, j : j + 1])
        gram_row, inv_row = gram[j : j + 1, :] * root, inv[j : j + 1, :] * root
        factor = jnp.where(row[:, 0:1] > j, gram[:, j : j + 1] * root, 0.0)
        gram = jnp.where(row == j, gram_row, gram - factor * gram_row)
        inv = jnp.where(row == j, inv_row, inv - factor * inv_row)
    o = jnp.dot(inv, flat, precision=lax.Precision.HIGHEST, preferred_element_type=f32)
    u_flat = jnp.concatenate([u[j] for j in range(WID // LANES)], axis=1)
    q = jnp.dot(inv, u_flat, precision=lax.Precision.HIGHEST, preferred_element_type=f32)
    basis[...] = o * math.sqrt(HID)
    inverse[...] = inv
    o_hi = (-o).astype(bf16)
    o_lo = (-o - o_hi.astype(f32)).astype(bf16)
    q_hi = q.astype(bf16)
    q_lo = (q - q_hi.astype(f32)).astype(bf16)
    lhs[...] = jnp.concatenate([o_hi, o_hi, o_lo, o_lo], axis=0)
    rhs[0:EVEN, :] = scaled[...]
    rhs[EVEN:AUG, :] = jnp.concatenate([q_hi, q_lo, q_hi, q_lo], axis=0)
    finish_rows()


def residual_rows(spans, lhs, rhs, act_h, out, held, buf, sem_in, sem_out):
    base, end = spans[0][0], spans[-1][1]

    def load(b):
        low, high = spans[b]
        return pltpu.make_async_copy(
            act_h.at[:, low:high], held.at[0:EVEN, low - base : high - base], sem_in.at[b]
        )

    def store(b):
        low, high = spans[b]
        return pltpu.make_async_copy(
            buf.at[b % 2, 0 : high - low, :], out.at[low:high, :], sem_out.at[b % 2]
        )

    for b in range(len(spans)):
        load(b).start()

    def compute():
        held[EVEN:AUG, :] = lhs[:, base:end]
        for b, (low, high) in enumerate(spans):
            load(b).wait()
            if b >= 2:
                store(b - 2).wait()
            buf[b % 2, 0 : high - low, :] = lax.dot_general(
                held[:, low - base : high - base],
                rhs[...],
                (((0,), (0,)), ((), ())),
                preferred_element_type=f32,
            ).astype(bf16)
            store(b).start()
        for b in range(max(0, len(spans) - 2), len(spans)):
            store(b).wait()

    return compute


def residual_scratch(spans):
    return [
        pltpu.VMEM((AUG, spans[-1][1] - spans[0][0]), bf16),
        pltpu.VMEM((2, max(high - low for low, high in spans), WID), bf16),
        pltpu.SemaphoreType.DMA((len(spans),)),
        pltpu.SemaphoreType.DMA((2,)),
    ]


def ortho(p, u, scaled, act_h):
    anywhere, vmem = pl.BlockSpec(memory_space=pl.ANY), pl.BlockSpec(memory_space=pltpu.VMEM)
    return pl.pallas_call(
        ortho_kernel,
        in_specs=[vmem, vmem, vmem, anywhere],
        out_specs=[vmem, vmem, vmem, vmem, anywhere],
        out_shape=[
            jax.ShapeDtypeStruct((RANK, HID), f32),
            jax.ShapeDtypeStruct((RANK, RANK), f32),
            jax.ShapeDtypeStruct((4 * RANK, HID), bf16),
            jax.ShapeDtypeStruct((AUG, WID), bf16),
            jax.ShapeDtypeStruct((HID, WID), bf16),
        ],
        scratch_shapes=residual_scratch(SPANS_A),
        compiler_params=pltpu.CompilerParams(vmem_limit_bytes=RES_LIMIT),
        cost_estimate=pl.CostEstimate(
            flops=2 * ROWS * HID * WID // 2, bytes_accessed=6 << 20, transcendentals=0
        ),
        name="ortho",
    )(p, u, scaled, act_h)


def residual_kernel(lhs, rhs, act_h, before, out, mark, held, buf, sem_in, sem_out):
    mark[...] = jnp.zeros_like(mark)
    residual_rows(SPANS_B, lhs, rhs, act_h, out, held, buf, sem_in, sem_out)()


def residual_of(lhs, rhs, act_h, before):
    anywhere, vmem = pl.BlockSpec(memory_space=pl.ANY), pl.BlockSpec(memory_space=pltpu.VMEM)
    return pl.pallas_call(
        residual_kernel,
        in_specs=[vmem, vmem, anywhere, anywhere],
        out_specs=[anywhere, vmem],
        out_shape=[jax.ShapeDtypeStruct((HID, WID), bf16), jax.ShapeDtypeStruct((RANK, LANES), f32)],
        scratch_shapes=residual_scratch(SPANS_B),
        input_output_aliases={3: 0},
        compiler_params=pltpu.CompilerParams(vmem_limit_bytes=RES_LIMIT),
        cost_estimate=pl.CostEstimate(flops=2 * ROWS * HID * WID, bytes_accessed=14 << 20, transcendentals=0),
        name="residual",
    )(lhs, rhs, act_h, before)


def finish_kernel(inverse, mine, other, q_out, *, devices):
    first = lax.axis_index("c") == 0
    half = WID // LANES // 2
    flat = jnp.concatenate(
        [jnp.where(first, mine[j], other[j]) for j in range(half)]
        + [jnp.where(first, other[j], mine[j]) for j in range(half)],
        axis=1,
    )
    q = jnp.dot(inverse[...], flat, precision=lax.Precision.HIGHEST, preferred_element_type=f32)
    q_out[...] = q * (1.0 / math.sqrt(devices))


def finish(inverse, mine, other, devices):
    return pl.pallas_call(
        functools.partial(finish_kernel, devices=devices),
        in_specs=[pl.BlockSpec(memory_space=pltpu.VMEM)] * 3,
        out_specs=pl.BlockSpec(memory_space=pltpu.VMEM),
        out_shape=jax.ShapeDtypeStruct((RANK, WID), f32),
        compiler_params=pltpu.CompilerParams(vmem_limit_bytes=4 << 20),
        name="finish",
    )(inverse, mine, other)


def total(v):
    terms = [v[i] for i in range(v.shape[0])]
    while len(terms) > 1:
        terms = [a + b for a, b in zip(terms[0::2], terms[1::2])]
    return terms[0]


def total_kernel(v, after, out):
    out[...] = total(v)


def total_after(v, after):
    return pl.pallas_call(
        total_kernel,
        in_specs=[pl.BlockSpec(memory_space=pltpu.VMEM)] * 2,
        out_specs=pl.BlockSpec(memory_space=pltpu.VMEM),
        out_shape=jax.ShapeDtypeStruct(v.shape[1:], f32),
        compiler_params=pltpu.CompilerParams(vmem_limit_bytes=4 << 20),
        name="total",
    )(v, after)


def spread_kernel(v, after, out):
    whole = total(v)
    for i in range(out.shape[0]):
        out[i] = whole


def spread(v, after, n):
    return pl.pallas_call(
        spread_kernel,
        in_specs=[pl.BlockSpec(memory_space=pltpu.VMEM)] * 2,
        out_specs=pl.BlockSpec(memory_space=pltpu.VMEM),
        out_shape=pltpu.VMEM((n,) + v.shape[1:], f32),
        compiler_params=pltpu.CompilerParams(vmem_limit_bytes=4 << 20),
        name="spread",
    )(v, after)


def add_spread_kernel(a, b, out):
    whole = a[...] + b[...]
    for i in range(out.shape[0]):
        out[i] = whole


def add_spread(a, b, n):
    return pl.pallas_call(
        add_spread_kernel,
        in_specs=[pl.BlockSpec(memory_space=pltpu.VMEM)] * 2,
        out_specs=pl.BlockSpec(memory_space=pltpu.VMEM),
        out_shape=pltpu.VMEM((n,) + a.shape, f32),
        compiler_params=pltpu.CompilerParams(vmem_limit_bytes=4 << 20),
        name="add_spread",
    )(a, b)


def swap(v):
    return lax.ppermute(v, "c", [(0, 1), (1, 0)])


def gather_all_to_all(v, axes, n):
    copies = jnp.broadcast_to(v[None], (n,) + v.shape).reshape((n * v.shape[0],) + v.shape[1:])
    return lax.all_to_all(copies, axes, 0, 0, tiled=True)


def body(pre_act, upstream, layer_scale, initial_q):
    act, act_h, scaled, p_local = front(pre_act, upstream, layer_scale.reshape(1, WID), initial_q)
    with jax.named_scope("sum_p"):
        part = total(lax.all_to_all(p_local, PLANE, 0, 0, tiled=True))
        part = total(gather_all_to_all(part[None], "z", 8))
        p_total = gather_all_to_all(part[None], PLANE, 32)
    u, keep, send = project(act, scaled, p_total)
    basis_out, inverse, lhs, rhs, early = ortho(p_total, u, scaled, act_h)
    residual, mark = residual_of(lhs, rhs, act_h, early)
    with jax.named_scope("sum_u"):
        t = add_spread(keep, swap(send), 16)
        t = lax.all_to_all(t, ("x", "y"), 0, 0, tiled=True)
        t = spread(t, inverse, 8)
        mine = total_after(lax.all_to_all(t, "z", 0, 0, tiled=True), mark)
        other = swap(mine)
    q_out = finish(inverse, mine, other, 256)
    return (basis_out, q_out, residual)


def solution(mesh):
    fine = Mesh(mesh.devices.reshape(8, 4, 4, 2), ("z", "x", "y", "c"))
    split = P(("z", "x", "y", "c"), None)
    return jax.shard_map(
        body, mesh=fine, in_specs=(split, split, P(), P()), out_specs=(P(), P(), split), check_vma=False
    )
```
